32 devices in a mesh: coil: 2 (over x), slab: 16 (over z, y, core).
Axes of the slice: x: 2, y: 2, z: 4, core: 2. Of those that a mesh axis runs over, the one named last changes fastest.
Arguments:
- solution: float32 [2, 1, 128, 192, 256], P(None, None, 'slab', 'coil'), may hold values from -6 to 6
- residual: float32 [2, 1, 128, 192, 256], P(None, None, 'slab', 'coil'), may hold values from -6 to 6
- direction: float32 [2, 1, 128, 192, 256], P(None, None, 'slab', 'coil'), may hold values from -6 to 6
- sens_maps: float32 [2, 16, 128, 192, 256], P(None, 'coil', 'slab'), may hold values from -1.05 to 1.05
- sampling: int32 [1, 128, 192], replicated, may hold values from 0 to 1, as said below
Outputs:
- next_solution: float32 [2, 1, 128, 192, 256], P(None, None, 'slab', 'coil')
- next_residual: float32 [2, 1, 128, 192, 256], P(None, None, 'slab', 'coil')
- next_direction: float32 [2, 1, 128, 192, 256], P(None, None, 'slab', 'coil')
The draws below stay inside these ranges and needn't reach their ends.
Inputs may be any that keep to these rules, and one draw needn't show every extreme that they name: sampling is 1 on every line whose kx lies within 4 of 0 or of 128 and whose ky lies within 4 of 0 or of 192.
All inputs are finite; a program needn't handle non-finite values.
Results may differ from the reference program's by a relative error of at most 0.00016.
Values sent between devices are 32-bit elements; how exact they have to be, the bound alone decides.
A program may use at most 192 MiB of HBM per device.

```python
import math
import jax
import jax.numpy as jnp
from jax import lax

NX = 128
NY = 192
NZ = 256
COILS = 16
FRAMES = 1
CALIB = 4


def smooth_factor(key, length, count):
    first_key, second_key = jax.random.split(key)
    weights = jax.random.uniform(first_key, (count, 3), jnp.float32, -1.0, 1.0)
    phases = jax.random.uniform(second_key, (count, 3), jnp.float32, -math.pi, math.pi)
    position = jnp.arange(length, dtype=jnp.float32) / length
    frequency = jnp.arange(3, dtype=jnp.float32)
    angles = 2.0 * math.pi * frequency[None, :, None] * position[None, None, :] + phases[:, :, None]
    profile = jnp.sum(weights[:, :, None] * jnp.cos(angles), axis=1)
    largest = jnp.maximum(jnp.max(jnp.abs(profile), axis=1, keepdims=True), 0.05)
    return profile / largest


def direction_parts(key):
    base_key = jax.random.fold_in(key, 11)
    x_key, y_key, scale_key, noise_key = jax.random.split(base_key, 4)
    along_x = smooth_factor(x_key, NX, 2 * FRAMES).reshape(2, FRAMES, NX)
    along_y = smooth_factor(y_key, NY, 2 * FRAMES).reshape(2, FRAMES, NY)
    smooth = 2.5 * along_x[:, :, :, None, None] * along_y[:, :, None, :, None]
    exponent = jax.random.uniform(scale_key, (1, FRAMES, 1, 1, NZ), jnp.float32, math.log(0.25), math.log(2.5))
    noise_part = jax.random.normal(noise_key, (2, FRAMES, NX, NY, NZ), jnp.float32)
    amplitude = jnp.exp(exponent)
    return jnp.clip(amplitude * smooth + noise_part, -6.0, 6.0)


def draw_direction(key, part):
    return direction_parts(key)


def draw_residual(key, part):
    searched = direction_parts(key)
    noise_key = jax.random.fold_in(key, 29)
    noise_part = jax.random.normal(noise_key, (2, FRAMES, NX, NY, NZ), jnp.float32)
    return jnp.clip(0.8 * searched + 0.6 * noise_part, -6.0, 6.0)


def draw_sens_maps(key, part):
    base_key = jax.random.fold_in(key, 23)
    x_key, y_key, rough_key = jax.random.split(base_key, 3)
    along_x = smooth_factor(x_key, NX, 2 * COILS).reshape(2, COILS, NX)
    along_y = smooth_factor(y_key, NY, 2 * COILS).reshape(2, COILS, NY)
    rough_factor = jax.random.uniform(rough_key, (1, COILS, NX, NY, NZ), jnp.float32, 0.5, 1.5)
    return 0.65 * along_x[:, :, :, None, None] * along_y[:, :, None, :, None] * rough_factor


def draw_sampling(key, part):
    base_key = jax.random.fold_in(key, 37)
    chosen = jax.random.randint(base_key, (FRAMES, NX, NY), 0, 3)
    index_x = jnp.arange(NX, dtype=jnp.int32)
    index_y = jnp.arange(NY, dtype=jnp.int32)
    near_x = (index_x <= CALIB) | (index_x >= NX - CALIB)
    near_y = (index_y <= CALIB) | (index_y >= NY - CALIB)
    centre = near_x[:, None] & near_y[None, :]
    return jnp.where(centre[None] | (chosen == 0), 1, 0).astype(jnp.int32)


def shard_levels(own_key, extent, cuts, low, top_value):
    level, own = 1.0, jax.random.fold_in(own_key, 6)
    for dim, parts in cuts:
        draws = jnp.exp(jax.random.uniform(jax.random.fold_in(own, dim), (parts,), jnp.float32, low / len(cuts), top_value / len(cuts)))
        level = level * jnp.repeat(draws, extent[dim] // parts).reshape([-1 if axis == dim else 1 for axis in range(len(extent))])
    return level


def scatter_about(stream_key, extent, width, most, shards=(), held_as=jnp.bfloat16):
    drawn = width * jax.random.normal(stream_key, extent, jnp.float32)
    if shards:
        drawn = drawn * shard_levels(stream_key, extent, shards, -0.22, 0.18)
    return jnp.clip(drawn, -most, most).astype(held_as)


def setup_inputs(seed: int = 0) -> dict:
    arg_keys = jax.random.split(jax.random.key(seed), 6)
    return {
        "solution": scatter_about(arg_keys[0], (2, FRAMES, NX, NY, NZ), 1.0, 6.0, ((2, 16), (3, 2)), jnp.float32),
        "residual": draw_residual(jax.random.fold_in(arg_keys[5], 71), 0),
        "direction": draw_direction(jax.random.fold_in(arg_keys[5], 71), 0),
        "sens_maps": draw_sens_maps(jax.random.fold_in(arg_keys[5], 71), 0),
        "sampling": draw_sampling(jax.random.fold_in(arg_keys[5], 71), 0),
    }


damping_weight = 0.5


def normal_map(direction, sens_maps, sampling):
    field = lax.complex(direction[0], direction[1])
    weight = sampling.astype(direction.dtype)[:, :, :, None]

    def add_coil(total, maps):
        coil = lax.complex(maps[0], maps[1])
        spectra = jnp.fft.fft2(coil[None] * field, axes=(1, 2), norm="ortho")
        back = jnp.fft.ifft2(spectra * weight, axes=(1, 2), norm="ortho")
        term = jnp.conj(coil)[None] * back
        return total + jnp.stack([jnp.real(term), jnp.imag(term)]), None

    total, unused = lax.scan(add_coil, jnp.zeros_like(direction), jnp.moveaxis(sens_maps, 1, 0))
    return total + damping_weight * direction


def reference(solution, residual, direction, sens_maps, sampling):
    image_ap = normal_map(direction, sens_maps, sampling)
    norm_now = jnp.sum(residual * residual)
    curvature = jnp.sum(direction * image_ap)
    alpha = norm_now / curvature
    next_solution = solution + alpha * direction
    next_residual = residual - alpha * image_ap
    fresh = jnp.sum(next_residual * next_residual)
    next_direction = next_residual + (fresh / norm_now) * direction
    return next_solution, next_residual, next_direction
```

```python
import math

import jax
import jax.numpy as jnp
import numpy as np
from jax import lax
from jax.experimental.layout import Layout, with_layout_constraint
from jax.sharding import PartitionSpec as P

damping_weight = 0.5
lanes = 128


def dft_table(length, inverse):
    index = np.arange(length)
    angle = (index[:, None] * index[None, :] % length) * (2.0 * math.pi / length)
    scale = 1.0 / math.sqrt(length)
    cosine = np.cos(angle) * scale
    sine = np.sin(angle) * scale
    if inverse:
        table = np.stack([np.stack([cosine, -sine]), np.stack([sine, cosine])])
    else:
        table = np.stack([np.stack([cosine, sine]), np.stack([-sine, cosine])])
    return jnp.asarray(table.astype(np.float32))


def second_pass(table, data):
    return jnp.einsum(
        "abky,wbcxy->wacxk",
        table,
        data,
        precision=lax.Precision.HIGH,
        preferred_element_type=jnp.float32,
    )


def first_pass(table, data):
    return jnp.einsum(
        "abkx,wbcxy->wacky",
        table,
        data,
        precision=lax.Precision.HIGH,
        preferred_element_type=jnp.float32,
    )


def row_major(data):
    return with_layout_constraint(data, Layout(major_to_minor=tuple(range(data.ndim))))


def pack(maps, groups):
    _, coils, rows, size_y, size_z = maps.shape
    split = maps.reshape(2, coils, rows, size_y, groups, size_z // groups)
    moved = jnp.transpose(split, (4, 0, 1, 2, 5, 3))
    whole = size_y // lanes * lanes
    if size_y - whole != lanes // 2:
        return moved
    tails = jnp.concatenate([moved[:, 0, ..., whole:], moved[:, 1, ..., whole:]], axis=-1)
    pieces = []
    for start in range(0, whole, lanes):
        pieces.append(moved[:, :, ..., start : start + lanes])
    return jnp.concatenate(pieces + [tails[:, None]], axis=1)


def unpack(data, size_y):
    groups, _, coils, rows, depth, _ = data.shape
    whole = size_y // lanes * lanes
    parts = []
    for part in range(2):
        if size_y - whole != lanes // 2:
            value = data[:, part]
        else:
            tail = data[:, -1, ..., part * (lanes // 2) : (part + 1) * (lanes // 2)]
            heads = [data[:, 2 * step + part] for step in range(whole // lanes)]
            value = jnp.concatenate(heads + [tail], axis=-1)
        moved = jnp.transpose(value, (3, 1, 0, 2, 4))
        parts.append(moved.reshape(depth, coils, groups * rows, size_y))
    return parts


def body(solution, residual, direction, sens_maps, sampling):
    size_x, size_y = sampling.shape[1:]
    size_z = direction.shape[-1]
    rows = direction.shape[2]
    coils = sens_maps.shape[1]
    groups = lax.axis_size("slab")
    members = lax.axis_size("coil")
    width = size_y // members
    everyone = groups * members
    first_fwd = dft_table(size_x, False)
    first_inv = dft_table(size_x, True)
    second_fwd = dft_table(size_y, False)
    second_inv = dft_table(size_y, True)
    weight = sampling[0].astype(jnp.float32)
    spans = 2 if size_z // groups >= 16 else 1
    depth = size_z // spans // groups

    moved = direction[:, 0].reshape(2, rows, width, spans, groups, depth)
    moved = jnp.transpose(moved, (4, 3, 0, 1, 5, 2))
    moved = lax.all_to_all(moved, "slab", split_axis=0, concat_axis=0, tiled=True)
    moved = lax.all_gather(moved, "coil", axis=5, tiled=True)
    moved = jnp.transpose(moved, (1, 4, 2, 0, 3, 5))
    fields = moved.reshape(spans, depth, 2, size_x, size_y)

    def apply(maps, field):
        real_map, imag_map = maps
        real_in = field[:, 0][:, None]
        imag_in = field[:, 1][:, None]
        data = jnp.stack(
            [real_map * real_in - imag_map * imag_in, real_map * imag_in + imag_map * real_in], axis=1
        )
        spectra = first_pass(first_fwd, second_pass(second_fwd, data)) * weight
        data = second_pass(second_inv, first_pass(first_inv, spectra))
        real_out = jnp.sum(real_map * data[:, 0] + imag_map * data[:, 1], axis=1)
        imag_out = jnp.sum(real_map * data[:, 1] - imag_map * data[:, 0], axis=1)
        return jnp.stack([real_out, imag_out], axis=1)

    combined = []
    for span in range(spans):
        extent = size_z // spans
        here = sens_maps[..., span * extent : (span + 1) * extent]
        half, quarter = coils // 2, coils // 4
        cuts = (0, half, half + quarter, coils) if span == spans - 1 else (0, half, coils)
        total = None
        for low, high in zip(cuts[:-1], cuts[1:]):
            sent = row_major(pack(here[:, low:high], groups))
            landed = lax.all_to_all(sent, "slab", split_axis=0, concat_axis=0, tiled=True)
            value = apply(unpack(landed, size_y), fields[span])
            total = value if total is None else total + value
        parts = total.reshape(depth, 2, size_x, members, width)
        parts = jnp.transpose(parts, (3, 2, 1, 0, 4))
        parts = lax.all_to_all(parts, "coil", split_axis=0, concat_axis=0, tiled=True)
        summed = jnp.sum(parts, axis=0).reshape(groups, rows, 2, depth, width)
        back = lax.all_to_all(summed, "slab", split_axis=0, concat_axis=0, tiled=True)
        combined.append(jnp.transpose(back, (2, 1, 4, 0, 3)).reshape(2, 1, rows, width, extent))
    image_ap = row_major(jnp.concatenate(combined, axis=-1)) + damping_weight * direction

    sums = jnp.stack(
        [
            jnp.sum(residual * residual),
            jnp.sum(direction * image_ap),
            jnp.sum(residual * image_ap),
            jnp.sum(image_ap * image_ap),
        ]
    )
    sums = jnp.broadcast_to(jnp.pad(sums, (0, lanes - 4)), (everyone, 1, lanes))
    sums = lax.all_to_all(sums, ("coil", "slab"), split_axis=0, concat_axis=0, tiled=True)
    sums = jnp.sum(sums, axis=(0, 1))
    norm_now, curvature, cross, square = sums[0], sums[1], sums[2], sums[3]
    alpha = norm_now / curvature
    fresh = norm_now - 2.0 * alpha * cross + alpha * alpha * square
    next_residual = residual - alpha * image_ap
    next_solution = solution + alpha * direction
    next_direction = next_residual + fresh / norm_now * direction
    return (next_solution, next_residual, next_direction)


def solution(mesh):
    field = P(None, None, "slab", "coil", None)
    in_specs = (field, field, field, P(None, "coil", "slab", None, None), P())
    out_specs = (field, field, field)
    return jax.shard_map(body, mesh=mesh, in_specs=in_specs, out_specs=out_specs, check_vma=False)
```
